32 devices in a mesh: row: 4 (over z), col: 8 (over y, x, core).
Axes of the slice: x: 2, y: 2, z: 4, core: 2. Of those that a mesh axis runs over, the one named last changes fastest.
Arguments:
- tokens: bfloat16 [512, 8192], P('col', 'row'), may hold values from -6 to 6
- out_grad: bfloat16 [512, 8192], P('col', 'row'), may hold values from -6 to 6
- gate_weight: bfloat16 [8192, 14336], P('row', 'col'), may hold values from -0.09375 to 0.09375
- up_weight: bfloat16 [8192, 14336], P('row', 'col'), may hold values from -0.09375 to 0.09375
- down_weight: bfloat16 [14336, 8192], P('col', 'row'), may hold values from -0.0625 to 0.0625
- gate_mask: int32 [64, 112], P('row', 'col'), may hold values 0 or 1
- up_mask: int32 [64, 112], P('row', 'col'), may hold values 0 or 1
- down_mask: int32 [112, 64], P('col', 'row'), may hold values 0 or 1
Outputs:
- output: bfloat16 [512, 8192], P('col', 'row')
- token_grad: bfloat16 [512, 8192], P('col', 'row')
- gate_grad: bfloat16 [8192, 14336], P('row', 'col')
- up_grad: bfloat16 [8192, 14336], P('row', 'col')
- down_grad: bfloat16 [14336, 8192], P('col', 'row')
The draws below stay inside these ranges and needn't reach their ends.
All inputs are finite; a program needn't handle non-finite values. No bound on the sum of `gate_mask` or of `up_mask` or of `down_mask` on one device may be relied on, other than what follows from the above.
Results may differ from the reference program's by a relative error of at most 0.03.
Values may be sent and summed in bfloat16 or wider, within the bound.
A program may use at most 128 MiB of HBM per device.

```python
import jax
import jax.numpy as jnp
from jax import lax

D = 8192
FF = 14336
BLK = 128
TOKENS = 512
N_ROW = 4


def with_ends(drawn, rng, smallest, high):
    index_at = [jax.random.randint(jax.random.fold_in(rng, axis), (), 0, length) for axis, length in enumerate(drawn.shape)]
    main_axis = drawn.shape.index(max(drawn.shape))
    next_to = index_at[:main_axis] + [(index_at[main_axis] + 1) % drawn.shape[main_axis]] + index_at[main_axis + 1:]
    return drawn.at[tuple(index_at)].set(smallest).at[tuple(next_to)].set(high)


def block_scale(stream_key, extent, cuts, low, high):
    factor_of = 1.0
    for position, blocks in cuts:
        draws = jax.random.uniform(jax.random.fold_in(jax.random.fold_in(stream_key, 6), position), (blocks,), jnp.float32, low / len(cuts), high / len(cuts))
        factor_of = factor_of * jnp.repeat(jnp.exp(draws), extent[position] // blocks).reshape((-1,) + (1,) * (len(extent) - 1 - position))
    return factor_of


def noise(key, extent, scale, bound, pieces=(), dtype=jnp.bfloat16):
    loudness = block_scale(key, extent, pieces, -0.22, 0.18) if pieces else 1.0
    result = jax.random.normal(key, extent, jnp.float32) * scale * loudness
    return jnp.minimum(jnp.maximum(result, -bound), bound).astype(dtype)


def setup_inputs(seed: int = 0) -> dict:
    arg_keys = jax.random.split(jax.random.key(seed), 9)
    tokens = noise(arg_keys[0], (TOKENS, D), 1.0, 6.0, ((0, 8), (1, 4)))
    out_grad = noise(arg_keys[1], (TOKENS, D), 1.0, 6.0, ((0, 8), (1, 4)))
    gate_weight = noise(arg_keys[2], (D, FF), (D // 2) ** -0.5, 0.09375, ((0, 4), (1, 8)))
    up_weight = noise(arg_keys[3], (D, FF), (D // 2) ** -0.5, 0.09375, ((0, 4), (1, 8)))
    down_weight = noise(arg_keys[4], (FF, D), (FF // 2) ** -0.5, 0.0625, ((0, 8), (1, 4)))
    gate_mask = with_ends((jax.random.randint(arg_keys[5], (D // BLK, FF // BLK), 0, 2) < 1).astype(jnp.int32), jax.random.fold_in(arg_keys[5], 1), 0, 1)
    up_mask = with_ends((jax.random.randint(arg_keys[6], (D // BLK, FF // BLK), 0, 2) < 1).astype(jnp.int32), jax.random.fold_in(arg_keys[6], 1), 0, 1)
    down_mask = with_ends((jax.random.randint(arg_keys[7], (FF // BLK, D // BLK), 0, 2) < 1).astype(jnp.int32), jax.random.fold_in(arg_keys[7], 1), 0, 1)
    return {"tokens": tokens, "out_grad": out_grad, "gate_weight": gate_weight, "up_weight": up_weight, "down_weight": down_weight, "gate_mask": gate_mask, "up_mask": up_mask, "down_mask": down_mask}


def widen(weight, keep_blocks):
    block_rows, block_cols = keep_blocks.shape
    block_size = weight.shape[0] // block_rows
    spread = jnp.broadcast_to(keep_blocks[:, None, :, None], (block_rows, block_size, block_cols, block_size))
    return weight * spread.reshape(weight.shape).astype(jnp.bfloat16)


def reference(tokens, out_grad, gate_weight, up_weight, down_weight, gate_mask, up_mask, down_mask):
    gate_masked = widen(gate_weight, gate_mask)
    up_masked = widen(up_weight, up_mask)
    down_masked = widen(down_weight, down_mask)
    piece = D // N_ROW
    hidden_width = gate_masked.shape[1]
    totals = jnp.zeros((tokens.shape[0], 3 * hidden_width), jnp.float32)
    for block_index in range(N_ROW):
        first = block_index * piece
        rows_x = tokens[:, first:first + piece]
        rows_g = out_grad[:, first:first + piece]
        term = jnp.concatenate([
            jnp.dot(rows_x, gate_masked[first:first + piece], preferred_element_type=jnp.float32),
            jnp.dot(rows_x, up_masked[first:first + piece], preferred_element_type=jnp.float32),
            jnp.dot(rows_g, down_masked[:, first:first + piece].T, preferred_element_type=jnp.float32)], axis=1)
        rounded = lax.optimization_barrier(term.astype(jnp.bfloat16))
        totals = totals + rounded.astype(jnp.float32)
    gate = totals[:, :hidden_width]
    up_part = totals[:, hidden_width:2 * hidden_width]
    hidden_grad = totals[:, 2 * hidden_width:]
    sigmoid_gate = jax.nn.sigmoid(gate)
    activated = gate * sigmoid_gate
    hidden = (activated * up_part).astype(jnp.bfloat16)
    gate_delta = (hidden_grad * up_part * sigmoid_gate * (1.0 + gate * (1.0 - sigmoid_gate))).astype(jnp.bfloat16)
    up_delta = (hidden_grad * activated).astype(jnp.bfloat16)
    output = jnp.dot(hidden, down_masked, preferred_element_type=jnp.float32).astype(jnp.bfloat16)
    token_grad = (jnp.dot(gate_delta, gate_masked.T, preferred_element_type=jnp.float32)
                  + jnp.dot(up_delta, up_masked.T, preferred_element_type=jnp.float32)).astype(jnp.bfloat16)
    down_grad = widen(jnp.dot(hidden.T, out_grad, preferred_element_type=jnp.float32).astype(jnp.bfloat16), down_mask)
    gate_grad = widen(jnp.dot(tokens.T, gate_delta, preferred_element_type=jnp.float32).astype(jnp.bfloat16), gate_mask)
    up_grad = widen(jnp.dot(tokens.T, up_delta, preferred_element_type=jnp.float32).astype(jnp.bfloat16), up_mask)
    return (output, token_grad, gate_grad, up_grad, down_grad)
```

```python
import functools

import jax
import jax.numpy as jnp
from jax import lax
from jax.experimental import pallas as pl
from jax.experimental.pallas import tpu as pltpu
from jax.sharding import PartitionSpec as P

MESH = pl.DeviceIdType.MESH
F32 = jnp.float32
BF16 = jnp.bfloat16
CHUNKS = 4


def contract_last(left, right):
    return lax.dot_general(
        left, right, (((1,), (1,)), ((), ())), preferred_element_type=F32
    )


def contract_first(left, right):
    return lax.dot_general(
        left, right, (((0,), (0,)), ((), ())), preferred_element_type=F32
    )


def exchange_kernel(
    n_row, n_col, fw, block,
    tokens_ref, grad_ref, gate_ref, up_ref, down_ref, gate_keep, up_keep, down_keep,
    out_ref, tgrad_ref, x_out, g_out, h_out, gd_out, ud_out,
    wg, wu, wd, x, g, held, part, acc, osend, orecv,
    w_sem, own_sem, cs_send, cs_recv, rs_send, rs_recv, ag_send, ag_recv,
    os_send, os_recv, xg_sem, h_sem,
):
    row = lax.axis_index("row")
    col = lax.axis_index("col")
    slabs = wg.shape[0]
    width = wg.shape[1]
    rows = x.shape[1]
    piece = rows // n_col
    units = CHUNKS * slabs
    pairs = units // 2
    last = n_row - 1

    def peer(offset):
        return lax.rem(col + offset, n_col)

    barrier = pltpu.get_barrier_semaphore()
    for offset in range(1, n_col):
        pl.semaphore_signal(barrier, inc=1, device_id=(row, peer(offset)), device_id_type=MESH)
    for offset in (1, n_row - 1):
        pl.semaphore_signal(
            barrier, inc=1, device_id=(lax.rem(row + offset, n_row), col), device_id_type=MESH
        )

    def weight_copies(s):
        at = pl.ds(s * fw, fw)
        return (
            pltpu.make_async_copy(gate_ref.at[:, at], wg.at[s], w_sem.at[0, s]),
            pltpu.make_async_copy(up_ref.at[:, at], wu.at[s], w_sem.at[1, s]),
            pltpu.make_async_copy(down_ref.at[at, :], wd.at[s], w_sem.at[2, s]),
        )

    def own_copies(t):
        src = pl.ds(t * piece, piece)
        dst = pl.ds(pl.multiple_of(col * piece, piece), piece)
        return [
            pltpu.make_async_copy(a.at[src], b.at[t, dst], own_sem.at[i, t])
            for i, (a, b) in enumerate(((tokens_ref, x), (grad_ref, g)))
        ]

    def gather_copies(t):
        src = pl.ds(pl.multiple_of(t * piece, piece), piece)
        dst = pl.ds(pl.multiple_of(col * piece, piece), piece)
        return [
            pltpu.make_async_remote_copy(
                src_ref=a.at[src],
                dst_ref=b.at[t, dst],
                send_sem=cs_send.at[i, t, offset - 1],
                recv_sem=cs_recv.at[i, t, offset - 1],
                device_id=(row, peer(offset)),
                device_id_type=MESH,
            )
            for offset in range(1, n_col)
            for i, (a, b) in enumerate(((tokens_ref, x), (grad_ref, g)))
        ]

    for t in range(CHUNKS):
        for copy in own_copies(t):
            copy.start()
    pl.semaphore_wait(barrier, n_col + 1)
    for copy in gather_copies(0):
        copy.start()
    for s in range(slabs):
        for copy in weight_copies(s):
            copy.start()

    def mask_slab(s, carry):
        for copy in weight_copies(s):
            copy.wait()
        for w, keep in ((wg, gate_keep), (wu, up_keep)):
            for b in range(width // block):
                at = pl.ds(b * block, block)
                w[s, at, :] = w[s, at, :] * keep[s, b : b + 1, :]
        for b in range(fw // block):
            at = pl.ds(b * block, block)
            wd[s, at, :] = wd[s, at, :] * down_keep[s, b : b + 1, :]
        return carry

    lax.fori_loop(0, slabs, mask_slab, 0)

    def take_chunk(t):
        for copy in own_copies(t):
            copy.wait()
        for copy in gather_copies(t):
            copy.wait()
        for i, (a, b) in enumerate(((x, x_out), (g, g_out))):
            at = pl.ds(pl.multiple_of(t * rows, rows), rows)
            pltpu.make_async_copy(a.at[t], b.at[at], xg_sem.at[i, t]).start()

    def where(u):
        t, s = u // slabs, lax.rem(u, slabs)
        return t, s, pl.ds(pl.multiple_of(t * rows, rows), rows)

    spans = [slice(i * fw, (i + 1) * fw) for i in range(3)]
    place = (last - row, row)
    ahead = (row - 1, row + 1)
    behind = (row + 1, row - 1)

    def forward(d, j):
        t, s, _ = where(2 * j + d)
        slot = lax.rem(j, 3)
        part[d, slot, :, spans[0]] = jnp.dot(
            x[t], wg[s], preferred_element_type=F32).astype(BF16)
        part[d, slot, :, spans[1]] = jnp.dot(
            x[t], wu[s], preferred_element_type=F32).astype(BF16)
        part[d, slot, :, spans[2]] = contract_last(g[t], wd[s]).astype(BF16)

    def sum_copy(d, j):
        _, s, at = where(2 * j + d)
        return pltpu.make_async_remote_copy(
            src_ref=part.at[d, lax.rem(j, 3)],
            dst_ref=held.at[s, at],
            send_sem=rs_send.at[d, j],
            recv_sem=rs_recv.at[d, j],
            device_id=(ahead[d], col),
            device_id_type=MESH,
        )

    def spread_copy(d, j):
        _, s, at = where(2 * j + d)
        return pltpu.make_async_remote_copy(
            src_ref=held.at[s, at],
            dst_ref=held.at[s, at],
            send_sem=ag_send.at[d, j],
            recv_sem=ag_recv.at[d, j],
            device_id=(behind[d], col),
            device_id_type=MESH,
        )

    def finish_sum(d, j):
        t, s, _ = where(2 * j + d)
        slot = lax.rem(j, 3)
        step = 16

        def some(r, carry):
            here = pl.ds(pl.multiple_of(r * step, step), step)
            there = pl.ds(pl.multiple_of(t * rows + r * step, step), step)
            gate, up, back = [
                part[d, slot, here, span].astype(F32) + held[s, there, span].astype(F32)
                for span in spans
            ]
            sig = jax.nn.sigmoid(gate)
            act = gate * sig
            held[s, there, spans[0]] = (act * up).astype(BF16)
            held[s, there, spans[1]] = (
                back * up * sig * (1.0 + gate * (1.0 - sig))
            ).astype(BF16)
            held[s, there, spans[2]] = (back * act).astype(BF16)
            return carry

        lax.fori_loop(0, rows // step, some, 0)

    def backward(d, j):
        t, s, at = where(2 * j + d)
        tile = min(512, width)
        hid, gd, ud = [held[s, at, span] for span in spans]
        for c in range(width // tile):
            cut = pl.ds(c * tile, tile)
            acc[t, 0, :, cut] += jnp.dot(hid, wd[s, :, cut], preferred_element_type=F32)
            acc[t, 1, :, cut] += contract_last(gd, wg[s, cut, :]) + contract_last(
                ud, wu[s, cut, :]
            )

    def result_copies(t):
        return [
            pltpu.make_async_remote_copy(
                src_ref=osend.at[
                    t, :, pl.ds(pl.multiple_of(peer(offset) * piece, piece), piece)
                ],
                dst_ref=orecv.at[t, offset - 1],
                send_sem=os_send.at[t, offset - 1],
                recv_sem=os_recv.at[t, offset - 1],
                device_id=(row, peer(offset)),
                device_id_type=MESH,
            )
            for offset in range(1, n_col)
        ]

    acc[...] = jnp.zeros_like(acc)
    take_chunk(0)
    for copy in gather_copies(1):
        copy.start()
    for d in range(2):
        @pl.when(place[d] == 0)
        def _():
            forward(d, 0)

    def step(k, carry):
        for d in range(2):
            j = k - place[d]

            @pl.when((j >= 0) & (j < pairs))
            def _():
                @pl.when(place[d] > 0)
                def _():
                    _, s, at = where(2 * j + d)
                    sum_copy(d, j).wait_recv()

                    @pl.when(place[d] < last)
                    def _():
                        slot = lax.rem(j, 3)
                        part[d, slot] = (
                            part[d, slot].astype(F32) + held[s, at, :].astype(F32)
                        ).astype(BF16)

                @pl.when(place[d] < last)
                def _():
                    sum_copy(d, j).start()

                @pl.when(place[d] == last)
                def _():
                    finish_sum(d, j)
                    spread_copy(d, j).start()

        for d in range(2):
            b = k - (2 * last - place[d])

            @pl.when((b >= 0) & (b < pairs) & (place[d] < last))
            def _():
                spread_copy(d, b).wait_recv()

                @pl.when(place[d] > 0)
                def _():
                    spread_copy(d, b).start()

        for t in range(1, CHUNKS):
            @pl.when(k == (t * slabs) // 2 - 1)
            def _():
                take_chunk(t)
                if t + 1 < CHUNKS:
                    for copy in gather_copies(t + 1):
                        copy.start()

        for d in range(2):
            j = k - place[d]

            @pl.when((j >= 1) & (j <= pairs) & (place[d] < last))
            def _():
                sum_copy(d, j - 1).wait_send()

            @pl.when((j >= -1) & (j < pairs - 1))
            def _():
                forward(d, j + 1)

        for d in range(2):
            b = k - (2 * last - place[d])

            @pl.when((b >= 0) & (b < pairs))
            def _():
                backward(d, b)

        done = jnp.int32(0)
        flag = jnp.int32(0)
        for t in range(CHUNKS):
            first, final = t * slabs, (t + 1) * slabs - 1
            ends = [max(u for u in (final - 1, final) if u % 2 == d) // 2 for d in range(2)]
            when = jnp.maximum(
                ends[0] + 2 * last - place[0], ends[1] + 2 * last - place[1]
            )
            hit = (when == k).astype(jnp.int32)
            done = done + hit * t
            flag = flag + hit

        @pl.when(flag > 0)
        def _():
            osend[done] = acc[done].astype(BF16)
            for copy in result_copies(done):
                copy.start()

        return carry

    lax.fori_loop(0, pairs + 2 * last, step, 0)

    h_copies = [
        pltpu.make_async_copy(
            held.at[s, :, spans[i]], ref.at[:, pl.ds(s * fw, fw)], h_sem.at[i, s]
        )
        for s in range(slabs)
        for i, ref in enumerate((h_out, gd_out, ud_out))
    ]
    for copy in h_copies:
        copy.start()

    def settle(j, carry):
        for d in range(2):
            @pl.when(place[d] > 0)
            def _():
                spread_copy(d, j).wait_send()

        return carry

    lax.fori_loop(0, pairs, settle, 0)

    def combine(t, carry):
        for copy in result_copies(t):
            copy.wait()
        mine = pl.ds(pl.multiple_of(col * piece, piece), piece)
        total = osend[t, :, mine].astype(F32)
        for offset in range(1, n_col):
            total = total + orecv[t, offset - 1].astype(F32)
        at = pl.ds(pl.multiple_of(t * piece, piece), piece)
        out_ref[at, :] = total[0].astype(BF16)
        tgrad_ref[at, :] = total[1].astype(BF16)
        for i, (a, b) in enumerate(((x, x_out), (g, g_out))):
            to = pl.ds(pl.multiple_of(t * rows, rows), rows)
            pltpu.make_async_copy(a.at[t], b.at[to], xg_sem.at[i, t]).wait()
        return carry

    lax.fori_loop(0, CHUNKS, combine, 0)
    for copy in h_copies:
        copy.wait()


def shards(n_row, n_col, tokens, out_grad, gate_weight, up_weight, down_weight,
           gate_mask, up_mask, down_mask):
    local, width = tokens.shape
    hidden = gate_weight.shape[1]
    block = width // gate_mask.shape[0]
    fw = 2 * block if hidden % (2 * block) == 0 else block
    slabs = hidden // fw
    rows = local * n_col // CHUNKS
    piece = local // CHUNKS
    pairs = CHUNKS * slabs // 2
    total = local * n_col

    def spread(mask):
        return jnp.repeat(mask.astype(BF16), block, axis=1)

    def by_slab(mask):
        wide = spread(mask)
        return wide.reshape(wide.shape[0], slabs, fw).transpose(1, 0, 2)

    gate_wide, up_wide, down_wide = spread(gate_mask), spread(up_mask), spread(down_mask)
    gate_keep, up_keep = by_slab(gate_mask), by_slab(up_mask)
    down_keep = down_wide.reshape(slabs, fw // block, width)

    any_spec = pl.BlockSpec(memory_space=pl.ANY)
    vmem_spec = pl.BlockSpec(memory_space=pltpu.VMEM)
    dma = pltpu.SemaphoreType.DMA
    shape = jax.ShapeDtypeStruct
    flops = 2 * total * width * hidden * 6
    output, token_grad, x, g, h, gd, ud = pl.pallas_call(
        functools.partial(exchange_kernel, n_row, n_col, fw, block),
        out_shape=[
            shape((local, width), BF16),
            shape((local, width), BF16),
            shape((total, width), BF16),
            shape((total, width), BF16),
            shape((total, hidden), BF16),
            shape((total, hidden), BF16),
            shape((total, hidden), BF16),
        ],
        in_specs=[any_spec] * 5 + [vmem_spec] * 3,
        out_specs=[vmem_spec] * 2 + [any_spec] * 5,
        scratch_shapes=[
            pltpu.VMEM((slabs, width, fw), BF16),
            pltpu.VMEM((slabs, width, fw), BF16),
            pltpu.VMEM((slabs, fw, width), BF16),
            pltpu.VMEM((CHUNKS, rows, width), BF16),
            pltpu.VMEM((CHUNKS, rows, width), BF16),
            pltpu.VMEM((slabs, total, 3 * fw), BF16),
            pltpu.VMEM((2, 3, rows, 3 * fw), BF16),
            pltpu.VMEM((CHUNKS, 2, rows, width), F32),
            pltpu.VMEM((CHUNKS, 2, rows, width), BF16),
            pltpu.VMEM((CHUNKS, n_col - 1, 2, piece, width), BF16),
            dma((3, slabs)),
            dma((2, CHUNKS)),
            dma((2, CHUNKS, n_col - 1)),
            dma((2, CHUNKS, n_col - 1)),
            dma((2, pairs)),
            dma((2, pairs)),
            dma((2, pairs)),
            dma((2, pairs)),
            dma((CHUNKS, n_col - 1)),
            dma((CHUNKS, n_col - 1)),
            dma((2, CHUNKS)),
            dma((3, slabs)),
        ],
        compiler_params=pltpu.CompilerParams(
            collective_id=0, has_side_effects=True, vmem_limit_bytes=60 * 2**20
        ),
        cost_estimate=pl.CostEstimate(
            flops=flops, bytes_accessed=3 * width * hidden * 2, transcendentals=0
        ),
    )(tokens, out_grad, gate_weight, up_weight, down_weight, gate_keep, up_keep, down_keep)

    def kept(grad, wide):
        tall = jnp.broadcast_to(wide[:, None, :], (wide.shape[0], block, wide.shape[1]))
        return grad.astype(BF16) * tall.reshape(grad.shape)

    down_grad = kept(contract_first(h, g), down_wide)
    gate_grad = kept(contract_first(x, gd), gate_wide)
    up_grad = kept(contract_first(x, ud), up_wide)
    return output, token_grad, gate_grad, up_grad, down_grad


def solution(mesh):
    spec = P("col", "row")
    flip = P("row", "col")
    in_specs = (spec, spec, flip, flip, spec, flip, flip, spec)
    out_specs = (spec, spec, flip, flip, spec)
    body = functools.partial(shards, mesh.shape["row"], mesh.shape["col"])
    return jax.shard_map(body, mesh=mesh, in_specs=in_specs, out_specs=out_specs, check_vma=False)
```

```python
import functools

import jax
import jax.numpy as jnp
from jax import lax
from jax.experimental import pallas as pl
from jax.experimental.pallas import tpu as pltpu
from jax.sharding import PartitionSpec as P

MESH = pl.DeviceIdType.MESH
F32 = jnp.float32
BF16 = jnp.bfloat16
CHUNKS = 4


def contract_last(left, right):
    return lax.dot_general(
        left, right, (((1,), (1,)), ((), ())), preferred_element_type=F32
    )


def contract_first(left, right):
    return lax.dot_general(
        left, right, (((0,), (0,)), ((), ())), preferred_element_type=F32
    )


def exchange_kernel(
    n_row, n_col, fw, block,
    tokens_ref, grad_ref, gate_ref, up_ref, down_ref, gate_keep, up_keep, down_keep,
    out_ref, tgrad_ref, xt_out, g_out, gd_out, ud_out, h_out,
    wgu, wd, x, g, xt, held, side, part, acc, osend, orecv,
    w_sem, own_sem, cs_send, cs_recv, rs_send, rs_recv, side_recv,
    ag_send, ag_recv, side_send, os_send, os_recv, xg_sem, h_sem,
):
    row = lax.axis_index("row")
    col = lax.axis_index("col")
    slabs = wgu.shape[0]
    width = wgu.shape[1]
    rows = x.shape[1]
    piece = rows // n_col
    units = CHUNKS * slabs
    pairs = units // 2
    reach = n_row // 2

    def peer(offset):
        return lax.rem(col + offset, n_col)

    barrier = pltpu.get_barrier_semaphore()
    for offset in range(1, n_col):
        pl.semaphore_signal(barrier, inc=1, device_id=(row, peer(offset)), device_id_type=MESH)
    for offset in (1, n_row - 1):
        pl.semaphore_signal(
            barrier, inc=1, device_id=(lax.rem(row + offset, n_row), col), device_id_type=MESH
        )

    def weight_copies(s):
        at = pl.ds(s * fw, fw)
        return (
            pltpu.make_async_copy(gate_ref.at[:, at], wgu.at[s, :, 0:fw], w_sem.at[0, s]),
            pltpu.make_async_copy(up_ref.at[:, at], wgu.at[s, :, fw : 2 * fw], w_sem.at[1, s]),
            pltpu.make_async_copy(down_ref.at[at, :], wd.at[s], w_sem.at[2, s]),
        )

    def own_copies(t):
        src = pl.ds(t * piece, piece)
        dst = pl.ds(pl.multiple_of(col * piece, piece), piece)
        return [
            pltpu.make_async_copy(a.at[src], b.at[t, dst], own_sem.at[i, t])
            for i, (a, b) in enumerate(((tokens_ref, x), (grad_ref, g)))
        ]

    def gather_copies(t):
        src = pl.ds(pl.multiple_of(t * piece, piece), piece)
        dst = pl.ds(pl.multiple_of(col * piece, piece), piece)
        return [
            pltpu.make_async_remote_copy(
                src_ref=a.at[src],
                dst_ref=b.at[t, dst],
                send_sem=cs_send.at[i, t, offset - 1],
                recv_sem=cs_recv.at[i, t, offset - 1],
                device_id=(row, peer(offset)),
                device_id_type=MESH,
            )
            for offset in range(1, n_col)
            for i, (a, b) in enumerate(((tokens_ref, x), (grad_ref, g)))
        ]

    for t in range(CHUNKS):
        for copy in own_copies(t):
            copy.start()
    pl.semaphore_wait(barrier, n_col + 1)
    for copy in gather_copies(0):
        copy.start()
    for s in range(slabs):
        for copy in weight_copies(s):
            copy.start()

    def widened(keep):
        return jnp.full((block, block), keep.astype(F32), F32).astype(BF16)

    def mask_slab(s, carry):
        for copy in weight_copies(s):
            copy.wait()
        for half, keep in enumerate((gate_keep, up_keep)):
            for n in range(fw // block):
                across = slice(half * fw + n * block, half * fw + (n + 1) * block)
                for b in range(width // block):
                    at = slice(b * block, (b + 1) * block)
                    wgu[s, at, across] = wgu[s, at, across] * widened(
                        keep[b, s * (fw // block) + n]
                    )
        for n in range(fw // block):
            at = slice(n * block, (n + 1) * block)
            for b in range(width // block):
                across = slice(b * block, (b + 1) * block)
                wd[s, at, across] = wd[s, at, across] * widened(
                    down_keep[s * (fw // block) + n, b]
                )
        return carry

    lax.fori_loop(0, slabs, mask_slab, 0)

    def take_chunk(t):
        for copy in own_copies(t):
            copy.wait()
        for copy in gather_copies(t):
            copy.wait()
        xt[t] = x[t].T
        for copy in keep_copies(t):
            copy.start()

    def keep_copies(t):
        at = pl.ds(pl.multiple_of(t * rows, rows), rows)
        return (
            pltpu.make_async_copy(xt.at[t], xt_out.at[:, at], xg_sem.at[0, t]),
            pltpu.make_async_copy(g.at[t], g_out.at[at], xg_sem.at[1, t]),
        )

    def where(u):
        t, s = u // slabs, lax.rem(u, slabs)
        return t, s, pl.ds(pl.multiple_of(t * rows, rows), rows)

    spans = [slice(i * fw, (i + 1) * fw) for i in range(3)]
    longer = (1, -1)
    place = (row - (reach - 1), reach - row)
    away = tuple(jnp.abs(p) for p in place)
    toward = tuple(jnp.where(place[d] > 0, row - longer[d], row + longer[d]) for d in range(2))
    beyond = tuple(jnp.where(place[d] >= 0, row + longer[d], row - longer[d]) for d in range(2))
    at_end = tuple((p == reach) | (p == 1 - reach) for p in place)

    def forward(d, j):
        t, s, _ = where(2 * j + d)
        slot = lax.rem(j, 3)
        part[d, slot, :, 0 : 2 * fw] = jnp.dot(
            x[t], wgu[s], preferred_element_type=F32).astype(BF16)
        part[d, slot, :, spans[2]] = contract_last(g[t], wd[s]).astype(BF16)

    def sum_copy(d, j):
        _, s, at = where(2 * j + d)
        return pltpu.make_async_remote_copy(
            src_ref=part.at[d, lax.rem(j, 3)],
            dst_ref=held.at[s, at],
            send_sem=rs_send.at[d, j],
            recv_sem=rs_recv.at[d, j],
            device_id=(toward[d], col),
            device_id_type=MESH,
        )

    def side_sum_copy(d, j):
        return pltpu.make_async_remote_copy(
            src_ref=part.at[d, lax.rem(j, 3)],
            dst_ref=side.at[j],
            send_sem=rs_send.at[d, j],
            recv_sem=side_recv.at[j],
            device_id=(toward[d], col),
            device_id_type=MESH,
        )

    def spread_copy(d, j):
        _, s, at = where(2 * j + d)
        return pltpu.make_async_remote_copy(
            src_ref=held.at[s, at],
            dst_ref=held.at[s, at],
            send_sem=ag_send.at[d, j],
            recv_sem=ag_recv.at[d, j],
            device_id=(beyond[d], col),
            device_id_type=MESH,
        )

    def side_spread_copy(d, j):
        _, s, at = where(2 * j + d)
        return pltpu.make_async_remote_copy(
            src_ref=held.at[s, at],
            dst_ref=held.at[s, at],
            send_sem=side_send.at[j],
            recv_sem=ag_recv.at[d, j],
            device_id=(row - longer[d], col),
            device_id_type=MESH,
        )

    def finish_sum(d, j):
        t, s, _ = where(2 * j + d)
        slot = lax.rem(j, 3)
        step = 16

        def some(r, carry):
            here = pl.ds(pl.multiple_of(r * step, step), step)
            there = pl.ds(pl.multiple_of(t * rows + r * step, step), step)
            gate, up, back = [
                part[d, slot, here, span].astype(F32)
                + held[s, there, span].astype(F32)
                + side[j, here, span].astype(F32)
                for span in spans
            ]
            sig = jax.nn.sigmoid(gate)
            act = gate * sig
            held[s, there, spans[0]] = (
                back * up * sig * (1.0 + gate * (1.0 - sig))
            ).astype(BF16)
            held[s, there, spans[1]] = (back * act).astype(BF16)
            held[s, there, spans[2]] = (act * up).astype(BF16)
            return carry

        lax.fori_loop(0, rows // step, some, 0)

    def backward(d, j):
        t, s, at = where(2 * j + d)
        tile = min(512, width)
        for c in range(width // tile):
            cut = pl.ds(c * tile, tile)
            acc[t, 0, :, cut] += jnp.dot(
                held[s, at, spans[2]], wd[s, :, cut], preferred_element_type=F32
            )
            acc[t, 1, :, cut] += contract_last(held[s, at, 0 : 2 * fw], wgu[s, cut, :])

    def result_copies(t):
        return [
            pltpu.make_async_remote_copy(
                src_ref=osend.at[
                    t, :, pl.ds(pl.multiple_of(peer(offset) * piece, piece), piece)
                ],
                dst_ref=orecv.at[t, offset - 1],
                send_sem=os_send.at[t, offset - 1],
                recv_sem=os_recv.at[t, offset - 1],
                device_id=(row, peer(offset)),
                device_id_type=MESH,
            )
            for offset in range(1, n_col)
        ]

    acc[...] = jnp.zeros_like(acc)
    take_chunk(0)
    for copy in gather_copies(1):
        copy.start()
    for d in range(2):
        @pl.when(away[d] == reach)
        def _():
            forward(d, 0)

    def step(k, carry):
        for d in range(2):
            j = k - (reach - away[d])

            @pl.when((j >= 0) & (j < pairs))
            def _():
                @pl.when((place[d] != 0) & jnp.logical_not(at_end[d]))
                def _():
                    _, s, at = where(2 * j + d)
                    slot = lax.rem(j, 3)
                    sum_copy(d, j).wait_recv()
                    part[d, slot] = (
                        part[d, slot].astype(F32) + held[s, at, :].astype(F32)
                    ).astype(BF16)

                @pl.when((place[d] > 0) | (place[d] < -1))
                def _():
                    sum_copy(d, j).start()

                @pl.when(place[d] == -1)
                def _():
                    side_sum_copy(d, j).start()

                @pl.when(place[d] == 0)
                def _():
                    sum_copy(d, j).wait_recv()
                    side_sum_copy(d, j).wait_recv()
                    finish_sum(d, j)
                    spread_copy(d, j).start()
                    side_spread_copy(d, j).start()

        for d in range(2):
            b = k - (reach + away[d])

            @pl.when((b >= 0) & (b < pairs) & (place[d] != 0))
            def _():
                spread_copy(d, b).wait_recv()

                @pl.when(jnp.logical_not(at_end[d]))
                def _():
                    spread_copy(d, b).start()

        for t in range(1, CHUNKS):
            @pl.when(k == (t * slabs) // 2 - 1)
            def _():
                take_chunk(t)
                if t + 1 < CHUNKS:
                    for copy in gather_copies(t + 1):
                        copy.start()

        for d in range(2):
            j = k - (reach - away[d])

            @pl.when((j >= 1) & (j <= pairs) & (place[d] != 0))
            def _():
                sum_copy(d, j - 1).wait_send()

            @pl.when((j >= -1) & (j < pairs - 1))
            def _():
                forward(d, j + 1)

        for d in range(2):
            b = k - (reach + away[d])

            @pl.when((b >= 0) & (b < pairs))
            def _():
                backward(d, b)

        done = jnp.int32(0)
        flag = jnp.int32(0)
        for t in range(CHUNKS):
            first, final = t * slabs, (t + 1) * slabs - 1
            ends = [max(u for u in (final - 1, final) if u % 2 == d) // 2 for d in range(2)]
            when = jnp.maximum(
                ends[0] + reach + away[0], ends[1] + reach + away[1]
            )
            hit = (when == k).astype(jnp.int32)
            done = done + hit * t
            flag = flag + hit

        @pl.when(flag > 0)
        def _():
            osend[done] = acc[done].astype(BF16)
            for copy in result_copies(done):
                copy.start()

        return carry

    lax.fori_loop(0, pairs + 2 * reach, step, 0)

    h_copies = [
        pltpu.make_async_copy(
            held.at[s, :, spans[i]], ref.at[:, pl.ds(s * fw, fw)], h_sem.at[i, s]
        )
        for s in range(slabs)
        for i, ref in enumerate((gd_out, ud_out, h_out))
    ]
    for copy in h_copies:
        copy.start()

    def settle(j, carry):
        for d in range(2):
            @pl.when(jnp.logical_not(at_end[d]))
            def _():
                spread_copy(d, j).wait_send()

            @pl.when(place[d] == 0)
            def _():
                side_spread_copy(d, j).wait_send()

        return carry

    lax.fori_loop(0, pairs, settle, 0)

    def combine(t, carry):
        for copy in result_copies(t):
            copy.wait()
        mine = pl.ds(pl.multiple_of(col * piece, piece), piece)
        total = osend[t, :, mine].astype(F32)
        for offset in range(1, n_col):
            total = total + orecv[t, offset - 1].astype(F32)
        at = pl.ds(pl.multiple_of(t * piece, piece), piece)
        out_ref[at, :] = total[0].astype(BF16)
        tgrad_ref[at, :] = total[1].astype(BF16)
        for copy in keep_copies(t):
            copy.wait()
        return carry

    lax.fori_loop(0, CHUNKS, combine, 0)
    for copy in h_copies:
        copy.wait()


def weight_grad_kernel(
    block, xt_ref, g_ref, gd_ref, ud_ref, h_ref, gate_keep, up_keep, down_keep,
    gate_out, up_out, down_out,
):
    s = pl.program_id(0)
    width, slab = gate_out.shape
    first = s * (slab // block)
    tile = min(512, width)
    for c in range(width // tile):
        cut = slice(c * tile, (c + 1) * tile)
        for delta, keep, out in ((gd_ref, gate_keep, gate_out), (ud_ref, up_keep, up_out)):
            grad = jnp.dot(xt_ref[cut, :], delta[...], preferred_element_type=F32)
            for b in range(tile // block):
                for n in range(slab // block):
                    at = slice(b * block, (b + 1) * block)
                    across = slice(n * block, (n + 1) * block)
                    kept = keep[c * (tile // block) + b, first + n].astype(F32)
                    out[c * tile + b * block : c * tile + (b + 1) * block, across] = (
                        grad[at, across] * kept
                    ).astype(BF16)
        grad = contract_first(h_ref[...], g_ref[:, cut])
        for b in range(tile // block):
            for n in range(slab // block):
                at = slice(n * block, (n + 1) * block)
                across = slice(b * block, (b + 1) * block)
                kept = down_keep[first + n, c * (tile // block) + b].astype(F32)
                down_out[at, c * tile + b * block : c * tile + (b + 1) * block] = (
                    grad[at, across] * kept
                ).astype(BF16)


def shards(n_row, n_col, tokens, out_grad, gate_weight, up_weight, down_weight,
           gate_mask, up_mask, down_mask):
    local, width = tokens.shape
    hidden = gate_weight.shape[1]
    block = width // gate_mask.shape[0]
    fw = 2 * block if hidden % (2 * block) == 0 else block
    slabs = hidden // fw
    rows = local * n_col // CHUNKS
    piece = local // CHUNKS
    pairs = CHUNKS * slabs // 2
    total = local * n_col

    any_spec = pl.BlockSpec(memory_space=pl.ANY)
    vmem_spec = pl.BlockSpec(memory_space=pltpu.VMEM)
    smem_spec = pl.BlockSpec(memory_space=pltpu.SMEM)
    dma = pltpu.SemaphoreType.DMA
    shape = jax.ShapeDtypeStruct
    flops = 2 * total * width * hidden * 6
    output, token_grad, xt, g, gd, ud, h = pl.pallas_call(
        functools.partial(exchange_kernel, n_row, n_col, fw, block),
        out_shape=[
            shape((local, width), BF16),
            shape((local, width), BF16),
            shape((width, total), BF16),
            shape((total, width), BF16),
            shape((total, hidden), BF16),
            shape((total, hidden), BF16),
            shape((total, hidden), BF16),
        ],
        in_specs=[any_spec] * 5 + [smem_spec] * 3,
        out_specs=[vmem_spec] * 2 + [any_spec] * 5,
        scratch_shapes=[
            pltpu.VMEM((slabs, width, 2 * fw), BF16),
            pltpu.VMEM((slabs, fw, width), BF16),
            pltpu.VMEM((CHUNKS, rows, width), BF16),
            pltpu.VMEM((CHUNKS, rows, width), BF16),
            pltpu.VMEM((CHUNKS, width, rows), BF16),
            pltpu.VMEM((slabs, total, 3 * fw), BF16),
            pltpu.VMEM((pairs, rows, 3 * fw), BF16),
            pltpu.VMEM((2, 3, rows, 3 * fw), BF16),
            pltpu.VMEM((CHUNKS, 2, rows, width), F32),
            pltpu.VMEM((CHUNKS, 2, rows, width), BF16),
            pltpu.VMEM((CHUNKS, n_col - 1, 2, piece, width), BF16),
            dma((3, slabs)),
            dma((2, CHUNKS)),
            dma((2, CHUNKS, n_col - 1)),
            dma((2, CHUNKS, n_col - 1)),
            dma((2, pairs)),
            dma((2, pairs)),
            dma((pairs,)),
            dma((2, pairs)),
            dma((2, pairs)),
            dma((pairs,)),
            dma((CHUNKS, n_col - 1)),
            dma((CHUNKS, n_col - 1)),
            dma((2, CHUNKS)),
            dma((3, slabs)),
        ],
        compiler_params=pltpu.CompilerParams(
            collective_id=0, has_side_effects=True, vmem_limit_bytes=60 * 2**20
        ),
        cost_estimate=pl.CostEstimate(
            flops=flops, bytes_accessed=3 * width * hidden * 2, transcendentals=0
        ),
    )(tokens, out_grad, gate_weight, up_weight, down_weight, gate_mask, up_mask, down_mask)

    slab = 2 * block if hidden % (2 * block) == 0 else block
    gate_grad, up_grad, down_grad = pl.pallas_call(
        functools.partial(weight_grad_kernel, block),
        grid=(hidden // slab,),
        out_shape=[
            shape((width, hidden), BF16),
            shape((width, hidden), BF16),
            shape((hidden, width), BF16),
        ],
        in_specs=[
            pl.BlockSpec((width, total), lambda s: (0, 0)),
            pl.BlockSpec((total, width), lambda s: (0, 0)),
        ]
        + [pl.BlockSpec((total, slab), lambda s: (0, s))] * 3
        + [smem_spec] * 3,
        out_specs=[
            pl.BlockSpec((width, slab), lambda s: (0, s)),
            pl.BlockSpec((width, slab), lambda s: (0, s)),
            pl.BlockSpec((slab, width), lambda s: (s, 0)),
        ],
        compiler_params=pltpu.CompilerParams(vmem_limit_bytes=48 * 2**20),
        cost_estimate=pl.CostEstimate(
            flops=flops // 2, bytes_accessed=3 * width * hidden * 2, transcendentals=0
        ),
    )(xt, g, gd, ud, h, gate_mask, up_mask, down_mask)
    return output, token_grad, gate_grad, up_grad, down_grad


def solution(mesh):
    spec = P("col", "row")
    flip = P("row", "col")
    in_specs = (spec, spec, flip, flip, spec, flip, flip, spec)
    out_specs = (spec, spec, flip, flip, spec)
    body = functools.partial(shards, mesh.shape["row"], mesh.shape["col"])
    return jax.shard_map(body, mesh=mesh, in_specs=in_specs, out_specs=out_specs, check_vma=False)
```

```python
import functools

import jax
import jax.numpy as jnp
from jax import lax
from jax.experimental import pallas as pl
from jax.experimental.pallas import tpu as pltpu
from jax.sharding import PartitionSpec as P

MESH = pl.DeviceIdType.MESH
F32 = jnp.float32
BF16 = jnp.bfloat16
CHUNKS = 4


def exchange_kernel(
    n_row, n_col, fw, block,
    tokens_ref, grad_ref, gate_ref, up_ref, down_ref, gate_keep, up_keep, down_keep,
    out_ref, tgrad_ref, xt_out, g_out, gd_out, ud_out, h_out,
    wgu, wd, x, g, xt, gt, held, side, part, acc, acc_t, osend, orecv,
    w_sem, own_sem, cs_send, cs_recv, rs_send, rs_recv, side_recv,
    ag_send, ag_recv, side_send, os_send, os_recv, xg_sem, h_sem,
):
    row = lax.axis_index("row")
    col = lax.axis_index("col")
    slabs = wgu.shape[0]
    width = wgu.shape[1]
    rows = x.shape[1]
    piece = rows // n_col
    units = CHUNKS * slabs
    pairs = units // 2
    reach = n_row // 2

    def peer(offset):
        return lax.rem(col + offset, n_col)

    barrier = pltpu.get_barrier_semaphore()
    for offset in range(1, n_col):
        pl.semaphore_signal(barrier, inc=1, device_id=(row, peer(offset)), device_id_type=MESH)
    for offset in (1, n_row - 1):
        pl.semaphore_signal(
            barrier, inc=1, device_id=(lax.rem(row + offset, n_row), col), device_id_type=MESH
        )

    def weight_copies(s):
        at = pl.ds(s * fw, fw)
        return (
            pltpu.make_async_copy(gate_ref.at[:, at], wgu.at[s, :, 0:fw], w_sem.at[0, s]),
            pltpu.make_async_copy(up_ref.at[:, at], wgu.at[s, :, fw : 2 * fw], w_sem.at[1, s]),
            pltpu.make_async_copy(down_ref.at[at, :], wd.at[s], w_sem.at[2, s]),
        )

    def own_copies(t):
        src = pl.ds(t * piece, piece)
        dst = pl.ds(pl.multiple_of(col * piece, piece), piece)
        return [
            pltpu.make_async_copy(a.at[src], b.at[t, dst], own_sem.at[i, t])
            for i, (a, b) in enumerate(((tokens_ref, x), (grad_ref, g)))
        ]

    def gather_copies(t):
        src = pl.ds(pl.multiple_of(t * piece, piece), piece)
        dst = pl.ds(pl.multiple_of(col * piece, piece), piece)
        return [
            pltpu.make_async_remote_copy(
                src_ref=a.at[src],
                dst_ref=b.at[t, dst],
                send_sem=cs_send.at[i, t, offset - 1],
                recv_sem=cs_recv.at[i, t, offset - 1],
                device_id=(row, peer(offset)),
                device_id_type=MESH,
            )
            for offset in range(1, n_col)
            for i, (a, b) in enumerate(((tokens_ref, x), (grad_ref, g)))
        ]

    for t in range(CHUNKS):
        for copy in own_copies(t):
            copy.start()
    pl.semaphore_wait(barrier, n_col + 1)
    for copy in gather_copies(0):
        copy.start()
    for s in range(slabs):
        for copy in weight_copies(s):
            copy.start()

    def widened(keep):
        return jnp.full((block, block), keep.astype(F32), F32).astype(BF16)

    def mask_slab(s, carry):
        for copy in weight_copies(s):
            copy.wait()
        for half, keep in enumerate((gate_keep, up_keep)):
            for n in range(fw // block):
                across = slice(half * fw + n * block, half * fw + (n + 1) * block)
                for b in range(width // block):
                    at = slice(b * block, (b + 1) * block)
                    wgu[s, at, across] = wgu[s, at, across] * widened(
                        keep[b, s * (fw // block) + n]
                    )
        for n in range(fw // block):
            at = slice(n * block, (n + 1) * block)
            for b in range(width // block):
                across = slice(b * block, (b + 1) * block)
                wd[s, at, across] = wd[s, at, across] * widened(
                    down_keep[s * (fw // block) + n, b]
                )
        return carry

    acc[...] = jnp.zeros_like(acc)
    acc_t[...] = jnp.zeros_like(acc_t)
    lax.fori_loop(0, 2, mask_slab, 0)

    def take_chunk(t):
        for copy in own_copies(t):
            copy.wait()
        for copy in gather_copies(t):
            copy.wait()
        xt[t] = x[t].T
        gt[t] = g[t].T
        for copy in keep_copies(t):
            copy.start()

    def keep_copies(t):
        at = pl.ds(pl.multiple_of(t * rows, rows), rows)
        return (
            pltpu.make_async_copy(xt.at[t], xt_out.at[:, at], xg_sem.at[0, t]),
            pltpu.make_async_copy(g.at[t], g_out.at[at], xg_sem.at[1, t]),
        )

    def where(u):
        t, s = u // slabs, lax.rem(u, slabs)
        return t, s, pl.ds(pl.multiple_of(t * rows, rows), rows)

    spans = [slice(i * fw, (i + 1) * fw) for i in range(3)]
    longer = (1, -1)
    place = (row - (reach - 1), reach - row)
    away = tuple(jnp.abs(p) for p in place)
    toward = tuple(jnp.where(place[d] > 0, row - longer[d], row + longer[d]) for d in range(2))
    beyond = tuple(jnp.where(place[d] >= 0, row + longer[d], row - longer[d]) for d in range(2))
    at_end = tuple((p == reach) | (p == 1 - reach) for p in place)

    def forward(d, j):
        t, s, _ = where(2 * j + d)
        slot = lax.rem(j, 3)
        part[d, slot, :, 0 : 2 * fw] = jnp.dot(
            x[t], wgu[s], preferred_element_type=F32).astype(BF16)
        back = jnp.dot(wd[s], gt[t], preferred_element_type=F32)
        part[d, slot, :, spans[2]] = back.T.astype(BF16)

    def sum_copy(d, j):
        _, s, at = where(2 * j + d)
        return pltpu.make_async_remote_copy(
            src_ref=part.at[d, lax.rem(j, 3)],
            dst_ref=held.at[s, at],
            send_sem=rs_send.at[d, j],
            recv_sem=rs_recv.at[d, j],
            device_id=(toward[d], col),
            device_id_type=MESH,
        )

    def side_sum_copy(d, j):
        return pltpu.make_async_remote_copy(
            src_ref=part.at[d, lax.rem(j, 3)],
            dst_ref=side.at[j],
            send_sem=rs_send.at[d, j],
            recv_sem=side_recv.at[j],
            device_id=(toward[d], col),
            device_id_type=MESH,
        )

    def spread_copy(d, j):
        _, s, at = where(2 * j + d)
        return pltpu.make_async_remote_copy(
            src_ref=held.at[s, at],
            dst_ref=held.at[s, at],
            send_sem=ag_send.at[d, j],
            recv_sem=ag_recv.at[d, j],
            device_id=(beyond[d], col),
            device_id_type=MESH,
        )

    def side_spread_copy(d, j):
        _, s, at = where(2 * j + d)
        return pltpu.make_async_remote_copy(
            src_ref=held.at[s, at],
            dst_ref=held.at[s, at],
            send_sem=side_send.at[j],
            recv_sem=ag_recv.at[d, j],
            device_id=(row - longer[d], col),
            device_id_type=MESH,
        )

    def finish_sum(d, j):
        t, s, _ = where(2 * j + d)
        slot = lax.rem(j, 3)
        step = 16

        def some(r, carry):
            here = pl.ds(pl.multiple_of(r * step, step), step)
            there = pl.ds(pl.multiple_of(t * rows + r * step, step), step)
            gate, up, back = [
                part[d, slot, here, span].astype(F32)
                + held[s, there, span].astype(F32)
                + side[j, here, span].astype(F32)
                for span in spans
            ]
            sig = jax.nn.sigmoid(gate)
            act = gate * sig
            held[s, there, spans[0]] = (
                back * up * sig * (1.0 + gate * (1.0 - sig))
            ).astype(BF16)
            held[s, there, spans[1]] = (back * act).astype(BF16)
            held[s, there, spans[2]] = (act * up).astype(BF16)
            return carry

        lax.fori_loop(0, rows // step, some, 0)

    def backward(d, j):
        t, s, at = where(2 * j + d)
        tile = min(512, width)
        deltas = held[s, at, 0 : 2 * fw].T
        for c in range(width // tile):
            cut = pl.ds(c * tile, tile)
            acc[t, :, cut] += jnp.dot(
                held[s, at, spans[2]], wd[s, :, cut], preferred_element_type=F32
            )
            acc_t[t, cut, :] += jnp.dot(wgu[s, cut, :], deltas, preferred_element_type=F32)

    def result_copies(t):
        return [
            pltpu.make_async_remote_copy(
                src_ref=osend.at[
                    t, :, pl.ds(pl.multiple_of(peer(offset) * piece, piece), piece)
                ],
                dst_ref=orecv.at[t, offset - 1],
                send_sem=os_send.at[t, offset - 1],
                recv_sem=os_recv.at[t, offset - 1],
                device_id=(row, peer(offset)),
                device_id_type=MESH,
            )
            for offset in range(1, n_col)
        ]

    take_chunk(0)
    for copy in gather_copies(1):
        copy.start()
    for d in range(2):
        @pl.when(away[d] == reach)
        def _():
            forward(d, 0)

    def step(k, carry):
        for d in range(2):
            j = k - (reach - away[d])

            @pl.when((j >= 0) & (j < pairs))
            def _():
                @pl.when((place[d] != 0) & jnp.logical_not(at_end[d]))
                def _():
                    _, s, at = where(2 * j + d)
                    slot = lax.rem(j, 3)
                    sum_copy(d, j).wait_recv()
                    part[d, slot] = (
                        part[d, slot].astype(F32) + held[s, at, :].astype(F32)
                    ).astype(BF16)

                @pl.when((place[d] > 0) | (place[d] < -1))
                def _():
                    sum_copy(d, j).start()

                @pl.when(place[d] == -1)
                def _():
                    side_sum_copy(d, j).start()

                @pl.when(place[d] == 0)
                def _():
                    sum_copy(d, j).wait_recv()
                    side_sum_copy(d, j).wait_recv()
                    finish_sum(d, j)
                    spread_copy(d, j).start()
                    side_spread_copy(d, j).start()

        for d in range(2):
            b = k - (reach + away[d])

            @pl.when((b >= 0) & (b < pairs) & (place[d] != 0))
            def _():
                spread_copy(d, b).wait_recv()

                @pl.when(jnp.logical_not(at_end[d]))
                def _():
                    spread_copy(d, b).start()

        for t in range(1, CHUNKS):
            @pl.when(k == (t * slabs) // 2 - 1)
            def _():
                take_chunk(t)
                if t + 1 < CHUNKS:
                    for copy in gather_copies(t + 1):
                        copy.start()

        for d in range(2):
            j = k - (reach - away[d])

            @pl.when((j >= 1) & (j <= pairs) & (place[d] != 0))
            def _():
                sum_copy(d, j - 1).wait_send()

            if d == 0:
                lax.fori_loop(
                    jnp.minimum(2 * k + 2, slabs),
                    jnp.minimum(2 * k + 4, slabs),
                    mask_slab,
                    0,
                )

            @pl.when((j >= -1) & (j < pairs - 1))
            def _():
                forward(d, j + 1)

        for d in range(2):
            b = k - (reach + away[d])

            @pl.when((b >= 0) & (b < pairs))
            def _():
                backward(d, b)

        done = jnp.int32(0)
        flag = jnp.int32(0)
        for t in range(CHUNKS):
            first, final = t * slabs, (t + 1) * slabs - 1
            ends = [max(u for u in (final - 1, final) if u % 2 == d) // 2 for d in range(2)]
            when = jnp.maximum(
                ends[0] + reach + away[0], ends[1] + reach + away[1]
            )
            hit = (when == k).astype(jnp.int32)
            done = done + hit * t
            flag = flag + hit

        @pl.when(flag > 0)
        def _():
            osend[done, 0] = acc[done].astype(BF16)
            osend[done, 1] = acc_t[done].astype(BF16).T
            for copy in result_copies(done):
                copy.start()

        return carry

    lax.fori_loop(0, pairs + 2 * reach, step, 0)

    h_copies = [
        pltpu.make_async_copy(
            held.at[s, :, spans[i]], ref.at[:, pl.ds(s * fw, fw)], h_sem.at[i, s]
        )
        for s in range(slabs)
        for i, ref in enumerate((gd_out, ud_out, h_out))
    ]
    for copy in h_copies:
        copy.start()

    def settle(j, carry):
        for d in range(2):
            @pl.when(jnp.logical_not(at_end[d]))
            def _():
                spread_copy(d, j).wait_send()

            @pl.when(place[d] == 0)
            def _():
                side_spread_copy(d, j).wait_send()

        return carry

    lax.fori_loop(0, pairs, settle, 0)

    def combine(t, carry):
        for copy in result_copies(t):
            copy.wait()
        mine = pl.ds(pl.multiple_of(col * piece, piece), piece)
        total = osend[t, :, mine].astype(F32)
        for offset in range(1, n_col):
            total = total + orecv[t, offset - 1].astype(F32)
        at = pl.ds(pl.multiple_of(t * piece, piece), piece)
        out_ref[at, :] = total[0].astype(BF16)
        tgrad_ref[at, :] = total[1].astype(BF16)
        for copy in keep_copies(t):
            copy.wait()
        return carry

    lax.fori_loop(0, CHUNKS, combine, 0)
    for copy in h_copies:
        copy.wait()


def weight_grad_kernel(
    block, xt_ref, g_ref, gd_ref, ud_ref, h_ref, gate_keep, up_keep, down_keep,
    gate_out, up_out, down_out,
):
    s = pl.program_id(0)
    width, slab = gate_out.shape
    first = s * (slab // block)
    tile = min(512, width)
    hidden_t = h_ref[...].T
    for c in range(width // tile):
        cut = slice(c * tile, (c + 1) * tile)
        for delta, keep, out in ((gd_ref, gate_keep, gate_out), (ud_ref, up_keep, up_out)):
            grad = jnp.dot(xt_ref[cut, :], delta[...], preferred_element_type=F32)
            for b in range(tile // block):
                for n in range(slab // block):
                    at = slice(b * block, (b + 1) * block)
                    across = slice(n * block, (n + 1) * block)
                    kept = keep[c * (tile // block) + b, first + n].astype(F32)
                    out[c * tile + b * block : c * tile + (b + 1) * block, across] = (
                        grad[at, across] * kept
                    ).astype(BF16)
        grad = jnp.dot(hidden_t, g_ref[:, cut], preferred_element_type=F32)
        for b in range(tile // block):
            for n in range(slab // block):
                at = slice(n * block, (n + 1) * block)
                across = slice(b * block, (b + 1) * block)
                kept = down_keep[first + n, c * (tile // block) + b].astype(F32)
                down_out[at, c * tile + b * block : c * tile + (b + 1) * block] = (
                    grad[at, across] * kept
                ).astype(BF16)


def shards(n_row, n_col, tokens, out_grad, gate_weight, up_weight, down_weight,
           gate_mask, up_mask, down_mask):
    local, width = tokens.shape
    hidden = gate_weight.shape[1]
    block = width // gate_mask.shape[0]
    fw = 2 * block if hidden % (2 * block) == 0 else block
    slabs = hidden // fw
    rows = local * n_col // CHUNKS
    piece = local // CHUNKS
    pairs = CHUNKS * slabs // 2
    total = local * n_col

    any_spec = pl.BlockSpec(memory_space=pl.ANY)
    vmem_spec = pl.BlockSpec(memory_space=pltpu.VMEM)
    smem_spec = pl.BlockSpec(memory_space=pltpu.SMEM)
    dma = pltpu.SemaphoreType.DMA
    shape = jax.ShapeDtypeStruct
    flops = 2 * total * width * hidden * 6
    output, token_grad, xt, g, gd, ud, h = pl.pallas_call(
        functools.partial(exchange_kernel, n_row, n_col, fw, block),
        out_shape=[
            shape((local, width), BF16),
            shape((local, width), BF16),
            shape((width, total), BF16),
            shape((total, width), BF16),
            shape((total, hidden), BF16),
            shape((total, hidden), BF16),
            shape((total, hidden), BF16),
        ],
        in_specs=[any_spec] * 5 + [smem_spec] * 3,
        out_specs=[vmem_spec] * 2 + [any_spec] * 5,
        scratch_shapes=[
            pltpu.VMEM((slabs, width, 2 * fw), BF16),
            pltpu.VMEM((slabs, fw, width), BF16),
            pltpu.VMEM((CHUNKS, rows, width), BF16),
            pltpu.VMEM((CHUNKS, rows, width), BF16),
            pltpu.VMEM((CHUNKS, width, rows), BF16),
            pltpu.VMEM((CHUNKS, width, rows), BF16),
            pltpu.VMEM((slabs, total, 3 * fw), BF16),
            pltpu.VMEM((pairs, rows, 3 * fw), BF16),
            pltpu.VMEM((2, 3, rows, 3 * fw), BF16),
            pltpu.VMEM((CHUNKS, rows, width), F32),
            pltpu.VMEM((CHUNKS, width, rows), F32),
            pltpu.VMEM((CHUNKS, 2, rows, width), BF16),
            pltpu.VMEM((CHUNKS, n_col - 1, 2, piece, width), BF16),
            dma((3, slabs)),
            dma((2, CHUNKS)),
            dma((2, CHUNKS, n_col - 1)),
            dma((2, CHUNKS, n_col - 1)),
            dma((2, pairs)),
            dma((2, pairs)),
            dma((pairs,)),
            dma((2, pairs)),
            dma((2, pairs)),
            dma((pairs,)),
            dma((CHUNKS, n_col - 1)),
            dma((CHUNKS, n_col - 1)),
            dma((2, CHUNKS)),
            dma((3, slabs)),
        ],
        compiler_params=pltpu.CompilerParams(
            collective_id=0, has_side_effects=True, vmem_limit_bytes=60 * 2**20
        ),
        cost_estimate=pl.CostEstimate(
            flops=flops, bytes_accessed=3 * width * hidden * 2, transcendentals=0
        ),
    )(tokens, out_grad, gate_weight, up_weight, down_weight, gate_mask, up_mask, down_mask)

    slab = 2 * block if hidden % (2 * block) == 0 else block
    gate_grad, up_grad, down_grad = pl.pallas_call(
        functools.partial(weight_grad_kernel, block),
        grid=(hidden // slab,),
        out_shape=[
            shape((width, hidden), BF16),
            shape((width, hidden), BF16),
            shape((hidden, width), BF16),
        ],
        in_specs=[
            pl.BlockSpec((width, total), lambda s: (0, 0)),
            pl.BlockSpec((total, width), lambda s: (0, 0)),
        ]
        + [pl.BlockSpec((total, slab), lambda s: (0, s))] * 3
        + [smem_spec] * 3,
        out_specs=[
            pl.BlockSpec((width, slab), lambda s: (0, s)),
            pl.BlockSpec((width, slab), lambda s: (0, s)),
            pl.BlockSpec((slab, width), lambda s: (s, 0)),
        ],
        compiler_params=pltpu.CompilerParams(vmem_limit_bytes=60 * 2**20),
        cost_estimate=pl.CostEstimate(
            flops=flops // 2, bytes_accessed=3 * width * hidden * 2, transcendentals=0
        ),
    )(xt, g, gd, ud, h, gate_mask, up_mask, down_mask)
    return output, token_grad, gate_grad, up_grad, down_grad


def solution(mesh):
    spec = P("col", "row")
    flip = P("row", "col")
    in_specs = (spec, spec, flip, flip, spec, flip, flip, spec)
    out_specs = (spec, spec, flip, flip, spec)
    body = functools.partial(shards, mesh.shape["row"], mesh.shape["col"])
    return jax.shard_map(body, mesh=mesh, in_specs=in_specs, out_specs=out_specs, check_vma=False)
```

```python
import functools

import jax
import jax.numpy as jnp
from jax import lax
from jax.experimental import pallas as pl
from jax.experimental.pallas import tpu as pltpu
from jax.sharding import PartitionSpec as P

MESH = pl.DeviceIdType.MESH
F32 = jnp.float32
BF16 = jnp.bfloat16
CHUNKS = 4
STRIDE = 2


def exchange_kernel(
    n_row, n_col, fw, block,
    tokens_ref, grad_ref, gate_ref, up_ref, down_ref, gate_keep, up_keep, down_keep,
    out_ref, tgrad_ref, xt_out, g_out, gd_out, ud_out, h_out,
    wgu, wd, x, g, xt, gt, held, side, part, acc, acc_t, osend, orecv,
    w_sem, own_sem, cs_send, cs_recv, rs_send, rs_recv, side_recv,
    ag_send, ag_recv, side_send, os_send, os_recv, xg_sem, h_sem,
):
    row = lax.axis_index("row")
    col = lax.axis_index("col")
    slabs = wgu.shape[0]
    width = wgu.shape[1]
    rows = x.shape[1]
    piece = rows // n_col
    units = CHUNKS * slabs
    pairs = units // 2
    reach = n_row // 2

    def peer(offset):
        return lax.rem(col + offset, n_col)

    barrier = pltpu.get_barrier_semaphore()
    for offset in range(1, n_col):
        pl.semaphore_signal(barrier, inc=1, device_id=(row, peer(offset)), device_id_type=MESH)
    for offset in (1, n_row - 1):
        pl.semaphore_signal(
            barrier, inc=1, device_id=(lax.rem(row + offset, n_row), col), device_id_type=MESH
        )

    def weight_copies(s):
        at = pl.ds(s * fw, fw)
        return (
            pltpu.make_async_copy(gate_ref.at[:, at], wgu.at[s, :, 0:fw], w_sem.at[0, s]),
            pltpu.make_async_copy(up_ref.at[:, at], wgu.at[s, :, fw : 2 * fw], w_sem.at[1, s]),
            pltpu.make_async_copy(down_ref.at[at, :], wd.at[s], w_sem.at[2, s]),
        )

    def own_copies(t):
        src = pl.ds(t * piece, piece)
        dst = pl.ds(pl.multiple_of(col * piece, piece), piece)
        return [
            pltpu.make_async_copy(a.at[src], b.at[t, dst], own_sem.at[i, t])
            for i, (a, b) in enumerate(((tokens_ref, x), (grad_ref, g)))
        ]

    def gather_copies(t):
        src = pl.ds(pl.multiple_of(t * piece, piece), piece)
        dst = pl.ds(pl.multiple_of(col * piece, piece), piece)
        return [
            pltpu.make_async_remote_copy(
                src_ref=a.at[src],
                dst_ref=b.at[t, dst],
                send_sem=cs_send.at[i, t, offset - 1],
                recv_sem=cs_recv.at[i, t, offset - 1],
                device_id=(row, peer(offset)),
                device_id_type=MESH,
            )
            for offset in range(1, n_col)
            for i, (a, b) in enumerate(((tokens_ref, x), (grad_ref, g)))
        ]

    for t in range(CHUNKS):
        for copy in own_copies(t):
            copy.start()
    pl.semaphore_wait(barrier, n_col + 1)
    for copy in gather_copies(0):
        copy.start()
    for s in range(slabs):
        for copy in weight_copies(s):
            copy.start()

    def widened(keep):
        return jnp.full((block, block), keep.astype(F32), F32).astype(BF16)

    def mask_slab(s, carry):
        for copy in weight_copies(s):
            copy.wait()
        for half, keep in enumerate((gate_keep, up_keep)):
            for n in range(fw // block):
                across = slice(half * fw + n * block, half * fw + (n + 1) * block)
                for b in range(width // block):
                    at = slice(b * block, (b + 1) * block)
                    wgu[s, at, across] = wgu[s, at, across] * widened(
                        keep[b, s * (fw // block) + n]
                    )
        for n in range(fw // block):
            at = slice(n * block, (n + 1) * block)
            for b in range(width // block):
                across = slice(b * block, (b + 1) * block)
                wd[s, at, across] = wd[s, at, across] * widened(
                    down_keep[s * (fw // block) + n, b]
                )
        return carry

    acc[...] = jnp.zeros_like(acc)
    acc_t[...] = jnp.zeros_like(acc_t)
    lax.fori_loop(0, 2, mask_slab, 0)

    def take_chunk(t):
        for copy in own_copies(t):
            copy.wait()
        for copy in gather_copies(t):
            copy.wait()
        xt[t] = x[t].T
        gt[t] = g[t].T
        for copy in keep_copies(t):
            copy.start()

    def keep_copies(t):
        at = pl.ds(pl.multiple_of(t * rows, rows), rows)
        return (
            pltpu.make_async_copy(xt.at[t], xt_out.at[:, at], xg_sem.at[0, t]),
            pltpu.make_async_copy(g.at[t], g_out.at[at], xg_sem.at[1, t]),
        )

    def where(u):
        t, s = u // slabs, lax.rem(u, slabs)
        return t, s, pl.ds(pl.multiple_of(t * rows, rows), rows)

    spans = [slice(i * fw, (i + 1) * fw) for i in range(3)]
    longer = (1, -1)
    place = (row - (reach - 1), reach - row)
    away = tuple(jnp.abs(p) for p in place)
    toward = tuple(jnp.where(place[d] > 0, row - longer[d], row + longer[d]) for d in range(2))
    beyond = tuple(jnp.where(place[d] >= 0, row + longer[d], row - longer[d]) for d in range(2))
    at_end = tuple((p == reach) | (p == 1 - reach) for p in place)

    def forward(d, j):
        t, s, _ = where(2 * j + d)
        slot = lax.rem(j, 4)
        part[d, slot, :, 0 : 2 * fw] = jnp.dot(
            x[t], wgu[s], preferred_element_type=F32).astype(BF16)
        back = jnp.dot(wd[s], gt[t], preferred_element_type=F32)
        part[d, slot, :, spans[2]] = back.T.astype(BF16)

    def sum_copy(d, j):
        _, s, at = where(2 * j + d)
        return pltpu.make_async_remote_copy(
            src_ref=part.at[d, lax.rem(j, 4)],
            dst_ref=held.at[s, at],
            send_sem=rs_send.at[d, j],
            recv_sem=rs_recv.at[d, j],
            device_id=(toward[d], col),
            device_id_type=MESH,
        )

    def side_sum_copy(d, j):
        return pltpu.make_async_remote_copy(
            src_ref=part.at[d, lax.rem(j, 4)],
            dst_ref=side.at[j],
            send_sem=rs_send.at[d, j],
            recv_sem=side_recv.at[j],
            device_id=(toward[d], col),
            device_id_type=MESH,
        )

    def spread_copy(d, j):
        _, s, at = where(2 * j + d)
        return pltpu.make_async_remote_copy(
            src_ref=held.at[s, at],
            dst_ref=held.at[s, at],
            send_sem=ag_send.at[d, j],
            recv_sem=ag_recv.at[d, j],
            device_id=(beyond[d], col),
            device_id_type=MESH,
        )

    def side_spread_copy(d, j):
        _, s, at = where(2 * j + d)
        return pltpu.make_async_remote_copy(
            src_ref=held.at[s, at],
            dst_ref=held.at[s, at],
            send_sem=side_send.at[j],
            recv_sem=ag_recv.at[d, j],
            device_id=(row - longer[d], col),
            device_id_type=MESH,
        )

    def finish_sum(d, j):
        t, s, _ = where(2 * j + d)
        slot = lax.rem(j, 4)
        step = 16

        def some(r, carry):
            here = pl.ds(pl.multiple_of(r * step, step), step)
            there = pl.ds(pl.multiple_of(t * rows + r * step, step), step)
            gate, up, back = [
                part[d, slot, here, span].astype(F32)
                + held[s, there, span].astype(F32)
                + side[j, here, span].astype(F32)
                for span in spans
            ]
            sig = jax.nn.sigmoid(gate)
            act = gate * sig
            held[s, there, spans[0]] = (
                back * up * sig * (1.0 + gate * (1.0 - sig))
            ).astype(BF16)
            held[s, there, spans[1]] = (back * act).astype(BF16)
            held[s, there, spans[2]] = (act * up).astype(BF16)
            return carry

        lax.fori_loop(0, rows // step, some, 0)

    def backward(d, j):
        t, s, at = where(2 * j + d)
        tile = min(512, width)
        deltas = held[s, at, 0 : 2 * fw].T
        for c in range(width // tile):
            cut = pl.ds(c * tile, tile)
            acc[t, :, cut] += jnp.dot(
                held[s, at, spans[2]], wd[s, :, cut], preferred_element_type=F32
            )
            acc_t[t, cut, :] += jnp.dot(wgu[s, cut, :], deltas, preferred_element_type=F32)

    def result_copies(t):
        return [
            pltpu.make_async_remote_copy(
                src_ref=osend.at[
                    t, :, pl.ds(pl.multiple_of(peer(offset) * piece, piece), piece)
                ],
                dst_ref=orecv.at[t, offset - 1],
                send_sem=os_send.at[t, offset - 1],
                recv_sem=os_recv.at[t, offset - 1],
                device_id=(row, peer(offset)),
                device_id_type=MESH,
            )
            for offset in range(1, n_col)
        ]

    take_chunk(0)
    for copy in gather_copies(1):
        copy.start()
    for d in range(2):
        @pl.when(away[d] == reach)
        def _():
            forward(d, 0)

    def step(k, carry):
        for d in range(2):
            j = k - STRIDE * (reach - away[d])

            @pl.when((j >= 0) & (j < pairs))
            def _():
                @pl.when((place[d] != 0) & jnp.logical_not(at_end[d]))
                def _():
                    _, s, at = where(2 * j + d)
                    slot = lax.rem(j, 4)
                    sum_copy(d, j).wait_recv()
                    part[d, slot] = (
                        part[d, slot].astype(F32) + held[s, at, :].astype(F32)
                    ).astype(BF16)

                @pl.when((place[d] > 0) | (place[d] < -1))
                def _():
                    sum_copy(d, j).start()

                @pl.when(place[d] == -1)
                def _():
                    side_sum_copy(d, j).start()

                @pl.when(place[d] == 0)
                def _():
                    sum_copy(d, j).wait_recv()
                    side_sum_copy(d, j).wait_recv()
                    finish_sum(d, j)
                    spread_copy(d, j).start()
                    side_spread_copy(d, j).start()

        for d in range(2):
            b = k - STRIDE * (reach + away[d])

            @pl.when((b >= 0) & (b < pairs) & (place[d] != 0))
            def _():
                spread_copy(d, b).wait_recv()

                @pl.when(jnp.logical_not(at_end[d]))
                def _():
                    spread_copy(d, b).start()

        for t in range(1, CHUNKS):
            @pl.when(k == (t * slabs) // 2 - 1)
            def _():
                take_chunk(t)
                if t + 1 < CHUNKS:
                    for copy in gather_copies(t + 1):
                        copy.start()

        for d in range(2):
            j = k - STRIDE * (reach - away[d])

            @pl.when((j >= 2) & (j < pairs + 2) & (place[d] != 0))
            def _():
                sum_copy(d, j - 2).wait_send()

            if d == 0:
                lax.fori_loop(
                    jnp.minimum(2 * k + 2, slabs),
                    jnp.minimum(2 * k + 4, slabs),
                    mask_slab,
                    0,
                )

            @pl.when((j >= -1) & (j < pairs - 1))
            def _():
                forward(d, j + 1)

        for d in range(2):
            b = k - STRIDE * (reach + away[d])

            @pl.when((b >= 0) & (b < pairs))
            def _():
                backward(d, b)

        done = jnp.int32(0)
        flag = jnp.int32(0)
        for t in range(CHUNKS):
            first, final = t * slabs, (t + 1) * slabs - 1
            ends = [max(u for u in (final - 1, final) if u % 2 == d) // 2 for d in range(2)]
            when = jnp.maximum(
                ends[0] + STRIDE * (reach + away[0]),
                ends[1] + STRIDE * (reach + away[1]),
            )
            hit = (when == k).astype(jnp.int32)
            done = done + hit * t
            flag = flag + hit

        @pl.when(flag > 0)
        def _():
            osend[done, 0] = acc[done].astype(BF16)
            osend[done, 1] = acc_t[done].astype(BF16).T
            for copy in result_copies(done):
                copy.start()

        return carry

    lax.fori_loop(0, pairs + 2 * STRIDE * reach, step, 0)

    h_copies = [
        pltpu.make_async_copy(
            held.at[s, :, spans[i]], ref.at[:, pl.ds(s * fw, fw)], h_sem.at[i, s]
        )
        for s in range(slabs)
        for i, ref in enumerate((gd_out, ud_out, h_out))
    ]
    for copy in h_copies:
        copy.start()

    def settle(j, carry):
        for d in range(2):
            @pl.when(jnp.logical_not(at_end[d]))
            def _():
                spread_copy(d, j).wait_send()

            @pl.when(place[d] == 0)
            def _():
                side_spread_copy(d, j).wait_send()

        return carry

    lax.fori_loop(0, pairs, settle, 0)

    def combine(t, carry):
        for copy in result_copies(t):
            copy.wait()
        mine = pl.ds(pl.multiple_of(col * piece, piece), piece)
        total = osend[t, :, mine].astype(F32)
        for offset in range(1, n_col):
            total = total + orecv[t, offset - 1].astype(F32)
        at = pl.ds(pl.multiple_of(t * piece, piece), piece)
        out_ref[at, :] = total[0].astype(BF16)
        tgrad_ref[at, :] = total[1].astype(BF16)
        for copy in keep_copies(t):
            copy.wait()
        return carry

    lax.fori_loop(0, CHUNKS, combine, 0)
    for copy in h_copies:
        copy.wait()


def weight_grad_kernel(
    block, xt_ref, g_ref, gd_ref, ud_ref, h_ref, gate_keep, up_keep, down_keep,
    gate_out, up_out, down_out,
):
    s = pl.program_id(0)
    width, slab = gate_out.shape
    first = s * (slab // block)
    tile = min(512, width)
    hidden_t = h_ref[...].T
    for c in range(width // tile):
        cut = slice(c * tile, (c + 1) * tile)
        for delta, keep, out in ((gd_ref, gate_keep, gate_out), (ud_ref, up_keep, up_out)):
            grad = jnp.dot(xt_ref[cut, :], delta[...], preferred_element_type=F32)
            for b in range(tile // block):
                for n in range(slab // block):
                    at = slice(b * block, (b + 1) * block)
                    across = slice(n * block, (n + 1) * block)
                    kept = keep[c * (tile // block) + b, first + n].astype(F32)
                    out[c * tile + b * block : c * tile + (b + 1) * block, across] = (
                        grad[at, across] * kept
                    ).astype(BF16)
        grad = jnp.dot(hidden_t, g_ref[:, cut], preferred_element_type=F32)
        for b in range(tile // block):
            for n in range(slab // block):
                at = slice(n * block, (n + 1) * block)
                across = slice(b * block, (b + 1) * block)
                kept = down_keep[first + n, c * (tile // block) + b].astype(F32)
                down_out[at, c * tile + b * block : c * tile + (b + 1) * block] = (
                    grad[at, across] * kept
                ).astype(BF16)


def shards(n_row, n_col, tokens, out_grad, gate_weight, up_weight, down_weight,
           gate_mask, up_mask, down_mask):
    local, width = tokens.shape
    hidden = gate_weight.shape[1]
    block = width // gate_mask.shape[0]
    fw = block
    slabs = hidden // fw
    rows = local * n_col // CHUNKS
    piece = local // CHUNKS
    pairs = CHUNKS * slabs // 2
    total = local * n_col

    any_spec = pl.BlockSpec(memory_space=pl.ANY)
    vmem_spec = pl.BlockSpec(memory_space=pltpu.VMEM)
    smem_spec = pl.BlockSpec(memory_space=pltpu.SMEM)
    dma = pltpu.SemaphoreType.DMA
    shape = jax.ShapeDtypeStruct
    flops = 2 * total * width * hidden * 6
    output, token_grad, xt, g, gd, ud, h = pl.pallas_call(
        functools.partial(exchange_kernel, n_row, n_col, fw, block),
        out_shape=[
            shape((local, width), BF16),
            shape((local, width), BF16),
            shape((width, total), BF16),
            shape((total, width), BF16),
            shape((total, hidden), BF16),
            shape((total, hidden), BF16),
            shape((total, hidden), BF16),
        ],
        in_specs=[any_spec] * 5 + [smem_spec] * 3,
        out_specs=[vmem_spec] * 2 + [any_spec] * 5,
        scratch_shapes=[
            pltpu.VMEM((slabs, width, 2 * fw), BF16),
            pltpu.VMEM((slabs, fw, width), BF16),
            pltpu.VMEM((CHUNKS, rows, width), BF16),
            pltpu.VMEM((CHUNKS, rows, width), BF16),
            pltpu.VMEM((CHUNKS, width, rows), BF16),
            pltpu.VMEM((CHUNKS, width, rows), BF16),
            pltpu.VMEM((slabs, total, 3 * fw), BF16),
            pltpu.VMEM((pairs, rows, 3 * fw), BF16),
            pltpu.VMEM((2, 4, rows, 3 * fw), BF16),
            pltpu.VMEM((CHUNKS, rows, width), F32),
            pltpu.VMEM((CHUNKS, width, rows), F32),
            pltpu.VMEM((CHUNKS, 2, rows, width), BF16),
            pltpu.VMEM((CHUNKS, n_col - 1, 2, piece, width), BF16),
            dma((3, slabs)),
            dma((2, CHUNKS)),
            dma((2, CHUNKS, n_col - 1)),
            dma((2, CHUNKS, n_col - 1)),
            dma((2, pairs)),
            dma((2, pairs)),
            dma((pairs,)),
            dma((2, pairs)),
            dma((2, pairs)),
            dma((pairs,)),
            dma((CHUNKS, n_col - 1)),
            dma((CHUNKS, n_col - 1)),
            dma((2, CHUNKS)),
            dma((3, slabs)),
        ],
        compiler_params=pltpu.CompilerParams(
            collective_id=0, has_side_effects=True, vmem_limit_bytes=60 * 2**20
        ),
        cost_estimate=pl.CostEstimate(
            flops=flops, bytes_accessed=3 * width * hidden * 2, transcendentals=0
        ),
    )(tokens, out_grad, gate_weight, up_weight, down_weight, gate_mask, up_mask, down_mask)

    slab = 2 * block if hidden % (2 * block) == 0 else block
    gate_grad, up_grad, down_grad = pl.pallas_call(
        functools.partial(weight_grad_kernel, block),
        grid=(hidden // slab,),
        out_shape=[
            shape((width, hidden), BF16),
            shape((width, hidden), BF16),
            shape((hidden, width), BF16),
        ],
        in_specs=[
            pl.BlockSpec((width, total), lambda s: (0, 0)),
            pl.BlockSpec((total, width), lambda s: (0, 0)),
        ]
        + [pl.BlockSpec((total, slab), lambda s: (0, s))] * 3
        + [smem_spec] * 3,
        out_specs=[
            pl.BlockSpec((width, slab), lambda s: (0, s)),
            pl.BlockSpec((width, slab), lambda s: (0, s)),
            pl.BlockSpec((slab, width), lambda s: (s, 0)),
        ],
        compiler_params=pltpu.CompilerParams(vmem_limit_bytes=60 * 2**20),
        cost_estimate=pl.CostEstimate(
            flops=flops // 2, bytes_accessed=3 * width * hidden * 2, transcendentals=0
        ),
    )(xt, g, gd, ud, h, gate_mask, up_mask, down_mask)
    return output, token_grad, gate_grad, up_grad, down_grad


def solution(mesh):
    spec = P("col", "row")
    flip = P("row", "col")
    in_specs = (spec, spec, flip, flip, spec, flip, flip, spec)
    out_specs = (spec, spec, flip, flip, spec)
    body = functools.partial(shards, mesh.shape["row"], mesh.shape["col"])
    return jax.shard_map(body, mesh=mesh, in_specs=in_specs, out_specs=out_specs, check_vma=False)
```
